32 devices in a mesh: walk: 4 (over x, core), chol: 8 (over z, y).
Axes of the slice: x: 2, y: 2, z: 4, core: 2. Of those that a mesh axis runs over, the one named last changes fastest.
Arguments:
- walkers: bfloat16 [8, 8, 1024, 256], P('walk', 'chol'), may hold values from -1 to 2
- counts: int32 [8, 8], P('walk', 'chol'), may hold values from 0 to 3, as said below
- slot_copy: int32 [8, 8], P('walk', 'chol'), may hold values from 0 to 7, as said below
- factors: bfloat16 [8, 256, 1024], P('chol'), may hold values from -1.5 to 1.5
Outputs:
- combed: bfloat16 [8, 8, 1024, 256], P('walk', 'chol')
- gradient: float32 [8, 8, 1024, 256], P('walk', 'chol')
The draws below stay inside these ranges and needn't reach their ends.
Inputs may be any that keep to these rules, and one draw needn't show every extreme that they name: In each population (column) the counts sum to 8. `slot_copy`: each column is a permutation of the copy numbers 0 to 7.
All inputs are finite; a program needn't handle non-finite values.
Results may differ from the reference program's by a relative error of at most 0.0068.
Values may be sent and summed in bfloat16 or wider, within the bound.
A program may use at most 64 MiB of HBM per device.

```python
import jax
import jax.numpy as jnp
from jax import lax

M = 1024
NEL = 256
CHOL_DEV = 1
NEWTON = 8
POP = 8
POPS = 8
CHOL = 8


def counts_column(column_key):
    shuffle = jax.random.permutation(column_key, POP)
    rank = jnp.zeros((POP,), jnp.int32).at[shuffle].set(jnp.arange(POP, dtype=jnp.int32))
    kinds = jax.random.randint(jax.random.fold_in(column_key, 7), (POP,), 0, 3)
    later = jnp.maximum(rank - 3, 0)
    pair_kind = kinds[later // 2]
    second = later % 2
    paired = jnp.where(pair_kind == 0, 1, jnp.where(pair_kind == 1, 2 - 2 * second, 2 * second))
    single = ((POP - 3) % 2 == 1) & (rank == POP - 1)
    return jnp.where(rank == 0, 3, jnp.where(rank < 3, 0, jnp.where(single, 1, paired))).astype(jnp.int32)


def draw_counts(key, part):

    def fold_column(column_index):
        return jax.random.fold_in(key, column_index)
    column_keys = jax.vmap(fold_column)(jnp.arange(POPS))
    columns = jax.vmap(counts_column)(column_keys)
    return columns.T


def draw_slot_copy(key, part):

    def permute_column(column_index):
        column_key = jax.random.fold_in(key, 100000 + column_index)
        return jax.random.permutation(column_key, POP).astype(jnp.int32)
    columns = jax.vmap(permute_column)(jnp.arange(POPS))
    return columns.T


def draw_walkers(key, part):
    key_top = jax.random.fold_in(key, 11)
    key_low = jax.random.fold_in(key, 12)
    noise_top = jnp.clip(jax.random.normal(key_top, (POP, POPS, NEL, NEL), jnp.float32), -4.0, 4.0)
    noise_low = jnp.clip(jax.random.normal(key_low, (POP, POPS, M - NEL, NEL), jnp.float32), -4.0, 4.0)
    spread = 1.0 / NEL ** 0.5
    skewed = 0.75 * spread * (noise_top - jnp.swapaxes(noise_top, -1, -2)) / 1.4142136
    identity = jnp.broadcast_to(jnp.eye(NEL, dtype=jnp.float32), skewed.shape)
    rotation = jnp.linalg.solve(identity - skewed, identity + skewed)
    upper = identity + 0.985 * rotation
    lower = spread * noise_low
    return jnp.concatenate([upper, lower], axis=2).astype(jnp.bfloat16)


def shard_levels(key, shape, split, least, largest):
    factor_of, own = 1.0, jax.random.fold_in(key, 6)
    for position, shards_of in split:
        draws = jnp.exp(jax.random.uniform(jax.random.fold_in(own, position), (shards_of,), jnp.float32, least / len(split), largest / len(split)))
        factor_of = factor_of * jnp.repeat(draws, shape[position] // shards_of).reshape([-1 if axis == position else 1 for axis in range(len(shape))])
    return factor_of


def noise(rng, dims, scale, bound, cuts=(), kind=jnp.bfloat16):
    loudness = shard_levels(rng, dims, cuts, -0.22, 0.18) if cuts else 1.0
    entries = jax.random.normal(rng, dims, jnp.float32) * scale * loudness
    return jnp.minimum(jnp.maximum(entries, -bound), bound).astype(kind)


def setup_inputs(seed: int = 0) -> dict:
    key_list = jax.random.split(jax.random.key(seed), 5)
    walkers = draw_walkers(jax.random.fold_in(key_list[4], 71), 0)
    counts = draw_counts(jax.random.fold_in(key_list[4], 71), 0)
    slot_copy = draw_slot_copy(jax.random.fold_in(key_list[4], 71), 0)
    factors = noise(key_list[3], (CHOL, NEL, M), ((4 * CHOL * NEL) ** -0.25), 1.5, ((0, 8),))
    return dict(walkers=walkers, counts=counts, slot_copy=slot_copy, factors=factors)


def reference(walkers, counts, slot_copy, factors):
    inclusive = jnp.cumsum(counts, axis=0).astype(jnp.int32)
    copy_index = jnp.arange(POP, dtype=jnp.int32)
    parent = jnp.sum((inclusive[None, :, :] <= copy_index[:, None, None]).astype(jnp.int32), axis=1).astype(jnp.int32)
    source = jnp.take_along_axis(parent, slot_copy, axis=0)
    column = jnp.arange(POPS, dtype=jnp.int32)[None, :]
    combed = walkers[source, column]
    intersection = combed[:, :, :NEL, :].astype(jnp.float32)
    identity = jnp.eye(NEL, dtype=jnp.float32)
    inverse = jnp.broadcast_to(identity, intersection.shape)
    for newton_step in range(NEWTON):
        product = jnp.einsum('pcij,pcjk->pcik', intersection, inverse, precision=lax.Precision.HIGHEST)
        inverse = jnp.einsum('pcij,pcjk->pcik', inverse, 2.0 * identity - product, precision=lax.Precision.HIGHEST)
    inverse_half = inverse.astype(jnp.bfloat16)
    green = jnp.einsum('pcmj,pcji->pcmi', combed.astype(jnp.float32), inverse_half.astype(jnp.float32)).astype(jnp.bfloat16)
    green_full = green.astype(jnp.float32)
    blocks = factors.reshape(POPS, CHOL_DEV, NEL, M)

    def accumulate(running, factor_block):
        block_full = factor_block.astype(jnp.float32)
        rotated = jnp.einsum('lrm,pcmq->pclrq', block_full, green_full).astype(jnp.bfloat16)
        rotated_full = lax.optimization_barrier(rotated).astype(jnp.float32)
        shard_grad = -jnp.einsum('lam,pclia->pcmi', block_full, rotated_full)
        shard_grad = lax.optimization_barrier(shard_grad.astype(jnp.bfloat16)).astype(jnp.float32)
        return (running + shard_grad, None)
    gradient, unused = lax.scan(accumulate, jnp.zeros(green.shape, jnp.float32), blocks)
    return (combed, gradient)
```

```python
import functools

import jax
import jax.numpy as jnp
from jax import lax
from jax.experimental import pallas as pl
from jax.experimental.pallas import tpu as pltpu
from jax.sharding import PartitionSpec as P

NEWTON = 8
MESH = pl.DeviceIdType.MESH
F32 = jnp.float32
BF16 = jnp.bfloat16


def kernel(nw, nc, cnt_ref, slot_ref, f_ref, w_ref, comb_ref, grad_ref, *scratch):
    per, rows, nel = w_ref.shape
    nch = rows // nel
    pop = nw * per
    arr = scratch[:nch]
    (full, cbuf, call, csm, ex, inv, green, racc, rt,
     csend, crecv, csem, wsem, rsem, fsem) = scratch[nch:]
    half = nc // 2
    chips = nw // 2
    part = rows // 4

    me = lax.axis_index("walk")
    col = lax.axis_index("chol")
    core = me % 2
    chip = me // 2
    sib = chip * 2 + (1 - core)
    odd = col % 2
    pos = (1 - odd) * (col // 2) + odd * (nc - 1 - col // 2)

    def at_pos(p):
        p = (p + 2 * nc) % nc
        hi = p // half
        return (1 - hi) * (2 * p) + hi * (2 * (nc - 1 - p) + 1)

    right, left = at_pos(pos + 1), at_pos(pos - 1)

    barrier = pltpu.get_barrier_semaphore()
    for k in range(1, nw):
        pl.semaphore_signal(barrier, inc=1, device_id=((me + k) % nw, col), device_id_type=MESH)
    for nb in (left, right):
        pl.semaphore_signal(barrier, inc=1, device_id=(me, nb), device_id_type=MESH)
    lane = lax.broadcasted_iota(jnp.int32, cbuf.shape, 1)
    packed = jnp.zeros(cbuf.shape, jnp.int32)
    for i in range(per):
        packed = jnp.where(lane == i, cnt_ref[i, 0], packed)
    cbuf[...] = packed
    pl.semaphore_wait(barrier, nw + 1)

    sends = []

    def remote(src, dst, ssem, rsem_, dev):
        return pltpu.make_async_remote_copy(
            src_ref=src, dst_ref=dst, send_sem=ssem, recv_sem=rsem_,
            device_id=dev, device_id_type=MESH)

    def go(copy):
        copy.start()
        sends.append(copy)

    def chunk(ch):
        return pl.ds(ch * nel, nel)

    def wx(ch, d):
        to = ((chip + d) % chips) * 2 + core
        return remote(w_ref.at[:, chunk(ch)], arr[ch].at[pl.ds(me * per, per)],
                      wsem.at[0, ch, d], wsem.at[1, ch, d], (to, col))

    def wx_in(ch, d):
        origin = ((chip - d + chips) % chips) * 2 + core
        return arr[ch].at[pl.ds(origin * per, per)]

    def ws(ch):
        return remote(w_ref.at[:, chunk(ch)], arr[ch].at[pl.ds(me * per, per)],
                      wsem.at[0, ch, 0], wsem.at[1, ch, 0], (sib, col))

    def wf(ch, d):
        block = wx_in(ch, d)
        return remote(block, block, wsem.at[2, ch, d], wsem.at[3, ch, d], (sib, col))

    def own(ch):
        return pltpu.make_async_copy(
            w_ref.at[:, chunk(ch)], arr[ch].at[pl.ds(me * per, per)], wsem.at[2, ch, 0])

    def landed(ref, sem):
        remote(ref, ref, sem, sem, (sib, col)).wait_recv()

    def walkers_in(ch):
        for d in range(1, chips):
            landed(wx_in(ch, d), wsem.at[1, ch, d])
            go(wf(ch, d))
        if ch + 2 < nch:
            for d in range(1, chips):
                go(wx(ch + 2, d))

    def walkers_all(ch):
        own(ch).wait()
        landed(arr[ch].at[pl.ds(sib * per, per)], wsem.at[1, ch, 0])
        for d in range(1, chips):
            origin = ((chip - d + chips) % chips) * 2 + (1 - core)
            landed(arr[ch].at[pl.ds(origin * per, per)], wsem.at[3, ch, d])

    for k in range(1, nw):
        go(remote(cbuf, call.at[me], csend.at[k], crecv.at[k], ((me + k) % nw, col)))
    for ch in range(min(2, nch)):
        for d in range(1, chips):
            go(wx(ch, d))
    for ch in range(nch):
        own(ch).start()
        go(ws(ch))

    for m in range(0, rows, nel):
        full[col, m:m + nel, :] = f_ref[:, m:m + nel].T

    def piece(origin, c, j):
        return full.at[origin, pl.ds((c * 2 + j) * part, part)]

    def ring(s, j, way):
        origin = at_pos(pos - (s - 1) if way == 0 else pos + (s - 1))
        block = piece(origin, core, j)
        return remote(block, block, rsem.at[0, way, s - 1, j], rsem.at[1, way, s - 1, j],
                      (me, right if way == 0 else left))

    def ways(s, j):
        return (0, 1) if s < half else (j,)

    def source_of(s, way):
        return at_pos(pos - s if way == 0 else pos + s)

    def factor_in(s, j):
        for way in ways(s, j):
            block = piece(source_of(s, way), core, j)
            landed(block, rsem.at[1, way, s - 1, j])
            if s < half and way in ways(s + 1, j):
                go(ring(s + 1, j, way))
            go(remote(block, block, fsem.at[0, way, s - 1, j], fsem.at[1, way, s - 1, j],
                      (sib, col)))

    def factor_all():
        for s in range(1, half + 1):
            for j in range(2):
                for way in ways(s, j):
                    landed(piece(source_of(s, way), 1 - core, j), fsem.at[1, way, s - 1, j])

    for j in range(2):
        for way in ways(1, j):
            go(ring(1, j, way))
    events = [(s, j) for s in range(1, half + 1) for j in range(2)]

    def pump(count):
        for _ in range(min(count, len(events))):
            factor_in(*events.pop(0))

    pump(2)
    walkers_in(0)

    call[me] = packed
    for k in range(1, nw):
        landed(call.at[(me - k + nw) % nw], crecv.at[k])
    to_smem = pltpu.make_async_copy(call, csm, csem.at[0])
    to_smem.start()
    to_smem.wait()
    wanted = [slot_ref[i, 0] for i in range(per)]
    chosen = [jnp.int32(0) for _ in range(per)]
    total = jnp.int32(0)
    for i in range(pop):
        total = total + csm[i // per, 0, i % per]
        for w in range(per):
            chosen[w] = chosen[w] + (total <= wanted[w]).astype(jnp.int32)
    chosen = [jnp.minimum(c, pop - 1) for c in chosen]

    def select(ch, w):
        block = arr[ch][chosen[w]]
        comb_ref[w, ch * nel:(ch + 1) * nel, :] = block
        return block.T

    eye = (lax.broadcasted_iota(jnp.int32, (nel, nel), 0)
           == lax.broadcasted_iota(jnp.int32, (nel, nel), 1)).astype(F32)
    walkers_all(0)
    tops = [select(0, w) for w in range(per)]
    for w in range(per):
        ex[w, :nel, :] = eye - tops[w].astype(F32)
        ex[w, nel:, :] = eye

    def newton(steps):
        def step(_, carry):
            for w in range(per):
                both = ex[w]
                prod = jnp.dot(both, both[:nel], precision=lax.Precision.HIGHEST,
                               preferred_element_type=F32)
                ex[w, :nel, :] = prod[:nel]
                ex[w, nel:, :] = both[nel:] + prod[nel:]
            return carry
        lax.fori_loop(0, steps, step, 0)

    def make_green(ch, flipped):
        for w in range(per):
            green[w * nel:(w + 1) * nel, ch * nel:(ch + 1) * nel] = jnp.dot(
                inv[w], flipped[w], preferred_element_type=F32).astype(BF16)

    def combine(ch):
        walkers_all(ch)
        make_green(ch, [select(ch, w) for w in range(per)])

    third = (NEWTON + 2) // 3
    newton(third)
    pump(1)
    newton(third)
    pump(1)
    walkers_in(1)
    newton(NEWTON - 2 * third)
    for w in range(per):
        inv[w] = ex[w, nel:, :].astype(BF16)
    make_green(0, tops)
    combine(1)
    pump(2)
    for ch in range(2, nch - 1):
        walkers_in(ch)
        combine(ch)
    pump(len(events))
    factor_all()
    lead = rows - nel

    def rotate_lead(l, carry):
        racc[l] = jnp.dot(green[:, :lead], full[l, :lead, :], preferred_element_type=F32)
        return carry

    lax.fori_loop(0, nc, rotate_lead, 0)
    walkers_in(nch - 1)
    combine(nch - 1)

    def rotate_last(l, carry):
        r = racc[l] + jnp.dot(green[:, lead:], full[l, lead:, :], preferred_element_type=F32)
        for w in range(per):
            rt[w, l] = r[w * nel:(w + 1) * nel].astype(BF16)
        return carry

    lax.fori_loop(0, nc, rotate_last, 0)

    def finish(b, carry):
        at = pl.ds(pl.multiple_of(b * nel, nel), nel)
        lhs = jnp.concatenate([full[l, at, :] for l in range(nc)], axis=1)
        for w in range(per):
            rhs = rt[w].reshape(nc * nel, nel)
            grad_ref[w, at, :] = -jnp.dot(lhs, rhs, preferred_element_type=F32)
        return carry

    lax.fori_loop(0, nch, finish, 0)
    for copy in sends:
        copy.wait_send()


def body(nw, nc, walkers, counts, slot_copy, factors):
    per, _, rows, nel = walkers.shape
    nch = rows // nel
    pop = nw * per
    vmem = pl.BlockSpec(memory_space=pltpu.VMEM)
    smem = pl.BlockSpec(memory_space=pltpu.SMEM)
    dma = pltpu.SemaphoreType.DMA
    half = nc // 2
    combed, grad = pl.pallas_call(
        functools.partial(kernel, nw, nc),
        out_shape=(
            jax.ShapeDtypeStruct((per, rows, nel), BF16),
            jax.ShapeDtypeStruct((per, rows, nel), F32),
        ),
        in_specs=[smem, smem, vmem, pl.BlockSpec(memory_space=pl.ANY)],
        out_specs=(vmem, vmem),
        scratch_shapes=[pltpu.VMEM((pop, nel, nel), BF16)] * nch + [
            pltpu.VMEM((nc, rows, nel), BF16),
            pltpu.VMEM((8, 128), jnp.int32),
            pltpu.VMEM((nw, 8, 128), jnp.int32),
            pltpu.SMEM((nw, 8, 128), jnp.int32),
            pltpu.VMEM((per, 2 * nel, nel), F32),
            pltpu.VMEM((per, nel, nel), BF16),
            pltpu.VMEM((per * nel, rows), BF16),
            pltpu.VMEM((nc, per * nel, nel), F32),
            pltpu.VMEM((per, nc, nel, nel), BF16),
            dma((nw,)),
            dma((nw,)),
            dma((1,)),
            dma((4, nch, nw // 2)),
            dma((2, 2, half, 2)),
            dma((2, 2, half, 2)),
        ],
        compiler_params=pltpu.CompilerParams(
            collective_id=0, has_side_effects=True, vmem_limit_bytes=56 << 20),
    )(counts, slot_copy, factors[0], walkers[:, 0])
    return combed[:, None], grad[:, None]


def solution(mesh):
    nw, nc = mesh.shape["walk"], mesh.shape["chol"]
    wide = P("walk", "chol", None, None)
    flat = P("walk", "chol")
    return jax.shard_map(
        functools.partial(body, nw, nc), mesh=mesh,
        in_specs=(wide, flat, flat, P("chol", None, None)),
        out_specs=(wide, wide), check_vma=False)
```

```python
import functools

import jax
import jax.numpy as jnp
from jax import lax
from jax.experimental import pallas as pl
from jax.experimental.pallas import tpu as pltpu
from jax.sharding import PartitionSpec as P

NEWTON = 8
MESH = pl.DeviceIdType.MESH
F32 = jnp.float32
BF16 = jnp.bfloat16


def kernel(nw, nc, cnt_ref, slot_ref, f_ref, w_ref, comb_out, grad_out, *scratch):
    per, rows, nel = w_ref.shape
    nch = rows // nel
    pop = nw * per
    arr = scratch[:nch]
    (full, cbuf, call, csm, ex, inv, green, racc, rt,
     comb_ref, grad_ref, osem, csend, crecv, csem, wsem, rsem, fsem) = scratch[nch:]
    half = nc // 2
    chips = nw // 2
    part = rows // 4

    me = lax.axis_index("walk")
    col = lax.axis_index("chol")
    core = me % 2
    chip = me // 2
    sib = chip * 2 + (1 - core)
    odd = col % 2
    pos = (1 - odd) * (col // 2) + odd * (nc - 1 - col // 2)

    def at_pos(p):
        p = (p + 2 * nc) % nc
        hi = p // half
        return (1 - hi) * (2 * p) + hi * (2 * (nc - 1 - p) + 1)

    right, left = at_pos(pos + 1), at_pos(pos - 1)

    barrier = pltpu.get_barrier_semaphore()
    for k in range(1, nw):
        pl.semaphore_signal(barrier, inc=1, device_id=((me + k) % nw, col), device_id_type=MESH)
    for nb in (left, right):
        pl.semaphore_signal(barrier, inc=1, device_id=(me, nb), device_id_type=MESH)
    lane = lax.broadcasted_iota(jnp.int32, cbuf.shape, 1)
    packed = jnp.zeros(cbuf.shape, jnp.int32)
    for i in range(per):
        packed = jnp.where(lane == i, cnt_ref[0, i], packed)
    cbuf[...] = packed
    pl.semaphore_wait(barrier, nw + 1)

    sends, outs = [], []

    def remote(src, dst, ssem, rsem_, dev):
        return pltpu.make_async_remote_copy(
            src_ref=src, dst_ref=dst, send_sem=ssem, recv_sem=rsem_,
            device_id=dev, device_id_type=MESH)

    def go(copy):
        copy.start()
        sends.append(copy)

    def chunk(ch):
        return pl.ds(ch * nel, nel)

    def wx(ch, d):
        to = ((chip + d) % chips) * 2 + core
        return remote(w_ref.at[:, chunk(ch)], arr[ch].at[pl.ds(me * per, per)],
                      wsem.at[0, ch, d], wsem.at[1, ch, d], (to, col))

    def wx_in(ch, d):
        origin = ((chip - d + chips) % chips) * 2 + core
        return arr[ch].at[pl.ds(origin * per, per)]

    def ws(ch):
        return remote(w_ref.at[:, chunk(ch)], arr[ch].at[pl.ds(me * per, per)],
                      wsem.at[0, ch, 0], wsem.at[1, ch, 0], (sib, col))

    def wf(ch, d):
        block = wx_in(ch, d)
        return remote(block, block, wsem.at[2, ch, d], wsem.at[3, ch, d], (sib, col))

    def own(ch):
        return pltpu.make_async_copy(
            w_ref.at[:, chunk(ch)], arr[ch].at[pl.ds(me * per, per)], wsem.at[2, ch, 0])

    def landed(ref, sem):
        remote(ref, ref, sem, sem, (sib, col)).wait_recv()

    def walkers_in(ch):
        for d in range(1, chips):
            landed(wx_in(ch, d), wsem.at[1, ch, d])
            go(wf(ch, d))
        if ch + 2 < nch:
            for d in range(1, chips):
                go(wx(ch + 2, d))

    def walkers_all(ch):
        own(ch).wait()
        landed(arr[ch].at[pl.ds(sib * per, per)], wsem.at[1, ch, 0])
        for d in range(1, chips):
            origin = ((chip - d + chips) % chips) * 2 + (1 - core)
            landed(arr[ch].at[pl.ds(origin * per, per)], wsem.at[3, ch, d])

    for k in range(1, nw):
        go(remote(cbuf, call.at[me], csend.at[k], crecv.at[k], ((me + k) % nw, col)))
    for d in range(1, chips):
        go(wx(0, d))
    for ch in range(nch):
        own(ch).start()
        go(ws(ch))

    for m in range(0, rows, nel):
        full[col, m:m + nel, :] = f_ref[:, m:m + nel].T

    def piece(origin, c, j):
        return full.at[origin, pl.ds((c * 2 + j) * part, part)]

    def ring(s, j, way):
        origin = at_pos(pos - (s - 1) if way == 0 else pos + (s - 1))
        block = piece(origin, core, j)
        return remote(block, block, rsem.at[0, way, s - 1, j], rsem.at[1, way, s - 1, j],
                      (me, right if way == 0 else left))

    def ways(s, j):
        return (0, 1) if s < half else (j,)

    def source_of(s, way):
        return at_pos(pos - s if way == 0 else pos + s)

    def factor_in(s, j):
        for way in ways(s, j):
            block = piece(source_of(s, way), core, j)
            landed(block, rsem.at[1, way, s - 1, j])
            if s < half and way in ways(s + 1, j):
                go(ring(s + 1, j, way))
            go(remote(block, block, fsem.at[0, way, s - 1, j], fsem.at[1, way, s - 1, j],
                      (sib, col)))

    def factor_all():
        for s in range(1, half + 1):
            for j in range(2):
                for way in ways(s, j):
                    landed(piece(source_of(s, way), 1 - core, j), fsem.at[1, way, s - 1, j])

    for j in range(2):
        for way in ways(1, j):
            go(ring(1, j, way))
    events = [(s, j) for s in range(1, half + 1) for j in range(2)]

    def pump(count):
        for _ in range(min(count, len(events))):
            factor_in(*events.pop(0))

    pump(1)
    for d in range(1, chips):
        go(wx(1, d))
    pump(1)
    walkers_in(0)

    call[me] = packed
    for k in range(1, nw):
        landed(call.at[(me - k + nw) % nw], crecv.at[k])
    to_smem = pltpu.make_async_copy(call, csm, csem.at[0])
    to_smem.start()
    to_smem.wait()
    wanted = [slot_ref[0, i] for i in range(per)]
    chosen = [jnp.int32(0) for _ in range(per)]
    total = jnp.int32(0)
    for i in range(pop):
        total = total + csm[i // per, 0, i % per]
        for w in range(per):
            chosen[w] = chosen[w] + (total <= wanted[w]).astype(jnp.int32)
    chosen = [jnp.minimum(c, pop - 1) for c in chosen]

    def select(ch, w):
        block = arr[ch][chosen[w]]
        comb_ref[w, ch * nel:(ch + 1) * nel, :] = block
        out = pltpu.make_async_copy(comb_ref.at[w, chunk(ch)], comb_out.at[w, chunk(ch)],
                                    osem.at[w, ch])
        out.start()
        outs.append(out)
        return block.T

    eye = (lax.broadcasted_iota(jnp.int32, (nel, nel), 0)
           == lax.broadcasted_iota(jnp.int32, (nel, nel), 1)).astype(F32)
    walkers_all(0)
    tops = [select(0, w) for w in range(per)]
    for w in range(per):
        ex[w, :nel, :] = eye - tops[w].astype(F32)
        ex[w, nel:, :] = eye

    def newton(steps):
        def step(_, carry):
            for w in range(per):
                both = ex[w]
                high = both.astype(BF16)
                low = (both - high.astype(F32)).astype(BF16)
                prod = (jnp.dot(high, high[:nel], preferred_element_type=F32)
                        + (jnp.dot(high, low[:nel], preferred_element_type=F32)
                           + jnp.dot(low, high[:nel], preferred_element_type=F32)))
                ex[w, :nel, :] = prod[:nel]
                ex[w, nel:, :] = both[nel:] + prod[nel:]
            return carry
        lax.fori_loop(0, steps, step, 0)

    def make_green(ch, flipped):
        for w in range(per):
            green[w * nel:(w + 1) * nel, ch * nel:(ch + 1) * nel] = jnp.dot(
                inv[w], flipped[w], preferred_element_type=F32).astype(BF16)

    def combine(ch):
        walkers_all(ch)
        make_green(ch, [select(ch, w) for w in range(per)])

    third = (NEWTON + 2) // 3
    newton(third)
    pump(1)
    newton(third)
    pump(1)
    walkers_in(1)
    newton(NEWTON - 2 * third)
    for w in range(per):
        inv[w] = ex[w, nel:, :].astype(BF16)
    make_green(0, tops)
    combine(1)
    pump(2)
    for ch in range(2, nch - 1):
        walkers_in(ch)
        combine(ch)
    pump(len(events))
    factor_all()
    lead = rows - nel

    def rotate_lead(l, carry):
        racc[l] = jnp.dot(green[:, :lead], full[l, :lead, :], preferred_element_type=F32)
        return carry

    lax.fori_loop(0, nc, rotate_lead, 0)
    walkers_in(nch - 1)
    combine(nch - 1)

    def rotate_last(l, carry):
        r = racc[l] + jnp.dot(green[:, lead:], full[l, lead:, :], preferred_element_type=F32)
        for w in range(per):
            rt[w, l] = r[w * nel:(w + 1) * nel].astype(BF16)
        return carry

    lax.fori_loop(0, nc, rotate_last, 0)

    for w in range(per):
        lhs = jnp.concatenate([full[l] for l in range(nc)], axis=1)
        rhs = rt[w].reshape(nc * nel, nel)
        grad_ref[w] = -jnp.dot(lhs, rhs, preferred_element_type=F32)
        out = pltpu.make_async_copy(grad_ref.at[w], grad_out.at[w], osem.at[w, nch])
        out.start()
        outs.append(out)
    for out in outs:
        out.wait()
    for copy in sends:
        copy.wait_send()


def body(nw, nc, walkers, counts, slot_copy, factors):
    per, _, rows, nel = walkers.shape
    nch = rows // nel
    pop = nw * per
    vmem = pl.BlockSpec(memory_space=pltpu.VMEM)
    smem = pl.BlockSpec(memory_space=pltpu.SMEM)
    dma = pltpu.SemaphoreType.DMA
    half = nc // 2
    combed, grad = pl.pallas_call(
        functools.partial(kernel, nw, nc),
        out_shape=(
            jax.ShapeDtypeStruct((per, rows, nel), BF16),
            jax.ShapeDtypeStruct((per, rows, nel), F32),
        ),
        in_specs=[smem, smem, vmem, pl.BlockSpec(memory_space=pl.ANY)],
        out_specs=(pl.BlockSpec(memory_space=pl.ANY),) * 2,
        scratch_shapes=[pltpu.VMEM((pop, nel, nel), BF16)] * nch + [
            pltpu.VMEM((nc, rows, nel), BF16),
            pltpu.VMEM((8, 128), jnp.int32),
            pltpu.VMEM((nw, 8, 128), jnp.int32),
            pltpu.SMEM((nw, 8, 128), jnp.int32),
            pltpu.VMEM((per, 2 * nel, nel), F32),
            pltpu.VMEM((per, nel, nel), BF16),
            pltpu.VMEM((per * nel, rows), BF16),
            pltpu.VMEM((nc, per * nel, nel), F32),
            pltpu.VMEM((per, nc, nel, nel), BF16),
            pltpu.VMEM((per, rows, nel), BF16),
            pltpu.VMEM((per, rows, nel), F32),
            dma((per, nch + 1)),
            dma((nw,)),
            dma((nw,)),
            dma((1,)),
            dma((4, nch, nw // 2)),
            dma((2, 2, half, 2)),
            dma((2, 2, half, 2)),
        ],
        compiler_params=pltpu.CompilerParams(
            collective_id=0, has_side_effects=True, vmem_limit_bytes=56 << 20),
    )(counts.T, slot_copy.T, factors[0], walkers[:, 0])
    return combed[:, None], grad[:, None]


def solution(mesh):
    nw, nc = mesh.shape["walk"], mesh.shape["chol"]
    wide = P("walk", "chol", None, None)
    flat = P("walk", "chol")
    return jax.shard_map(
        functools.partial(body, nw, nc), mesh=mesh,
        in_specs=(wide, flat, flat, P("chol", None, None)),
        out_specs=(wide, wide), check_vma=False)
```

```python
import functools

import jax
import jax.numpy as jnp
from jax import lax
from jax.experimental import pallas as pl
from jax.experimental.pallas import tpu as pltpu
from jax.sharding import PartitionSpec as P

NEWTON = 8
MESH = pl.DeviceIdType.MESH
F32 = jnp.float32
BF16 = jnp.bfloat16


def kernel(nw, nc, cnt_ref, slot_ref, f_ref, w_ref, comb_out, grad_out, *scratch):
    per, rows, nel = w_ref.shape
    nch = rows // nel
    pop = nw * per
    arr = scratch[:nch]
    (full, cbuf, call, csm, ex, inv, green, racc, rt,
     comb_ref, grad_ref, osem, csend, crecv, csem, wsem, xsem, rsem, fsem) = scratch[nch:]
    half = nc // 2
    chips = nw // 2
    part = rows // 4

    me = lax.axis_index("walk")
    col = lax.axis_index("chol")
    core = me % 2
    chip = me // 2
    sib = chip * 2 + (1 - core)
    odd = col % 2
    pos = (1 - odd) * (col // 2) + odd * (nc - 1 - col // 2)

    def at_pos(p):
        p = (p + 2 * nc) % nc
        hi = p // half
        return (1 - hi) * (2 * p) + hi * (2 * (nc - 1 - p) + 1)

    right, left = at_pos(pos + 1), at_pos(pos - 1)

    barrier = pltpu.get_barrier_semaphore()
    for k in range(1, nw):
        pl.semaphore_signal(barrier, inc=1, device_id=((me + k) % nw, col), device_id_type=MESH)
    for nb in (left, right):
        pl.semaphore_signal(barrier, inc=1, device_id=(me, nb), device_id_type=MESH)
    lane = lax.broadcasted_iota(jnp.int32, cbuf.shape, 1)
    packed = jnp.zeros(cbuf.shape, jnp.int32)
    for i in range(per):
        packed = jnp.where(lane == i, cnt_ref[0, i], packed)
    cbuf[...] = packed
    pl.semaphore_wait(barrier, nw + 1)

    sends, outs = [], []

    def remote(src, dst, ssem, rsem_, dev):
        return pltpu.make_async_remote_copy(
            src_ref=src, dst_ref=dst, send_sem=ssem, recv_sem=rsem_,
            device_id=dev, device_id_type=MESH)

    def go(copy):
        copy.start()
        sends.append(copy)

    def chunk(ch):
        return pl.ds(ch * nel, nel)

    def wx(ch, d, h):
        to = ((chip + d) % chips) * 2 + core
        at = pl.ds(h * (nel // 2), nel // 2)
        return remote(w_ref.at[:, pl.ds(ch * nel + h * (nel // 2), nel // 2)],
                      arr[ch].at[pl.ds(me * per, per), at],
                      xsem.at[0, ch, d, h], xsem.at[1, ch, d, h], (to, col))

    def wx_in(ch, d, h):
        origin = ((chip - d + chips) % chips) * 2 + core
        return arr[ch].at[pl.ds(origin * per, per), pl.ds(h * (nel // 2), nel // 2)]

    def ws(ch):
        return remote(w_ref.at[:, chunk(ch)], arr[ch].at[pl.ds(me * per, per)],
                      wsem.at[0, ch, 0], wsem.at[1, ch, 0], (sib, col))

    def wf(ch, d, h):
        block = wx_in(ch, d, h)
        return remote(block, block, xsem.at[2, ch, d, h], xsem.at[3, ch, d, h], (sib, col))

    def own(ch):
        return pltpu.make_async_copy(
            w_ref.at[:, chunk(ch)], arr[ch].at[pl.ds(me * per, per)], wsem.at[2, ch, 0])

    def landed(ref, sem):
        remote(ref, ref, sem, sem, (sib, col)).wait_recv()

    def send_chunk(ch, d):
        for h in range(2):
            go(wx(ch, d, h))

    def walkers_in(ch):
        for d in range(1, chips):
            for h in range(2):
                landed(wx_in(ch, d, h), xsem.at[1, ch, d, h])
                go(wf(ch, d, h))
        if ch + 2 < nch:
            for d in range(1, chips):
                send_chunk(ch + 2, d)

    def walkers_all(ch):
        own(ch).wait()
        landed(arr[ch].at[pl.ds(sib * per, per)], wsem.at[1, ch, 0])
        for d in range(1, chips):
            origin = ((chip - d + chips) % chips) * 2 + (1 - core)
            for h in range(2):
                landed(arr[ch].at[pl.ds(origin * per, per), pl.ds(h * (nel // 2), nel // 2)],
                       xsem.at[3, ch, d, h])

    for k in range(1, nw):
        go(remote(cbuf, call.at[me], csend.at[k], crecv.at[k], ((me + k) % nw, col)))
    for d in range(1, chips):
        send_chunk(0, d)
    for ch in range(nch):
        own(ch).start()
        go(ws(ch))

    for m in range(0, rows, nel):
        full[col, m:m + nel, :] = f_ref[:, m:m + nel].T

    def piece(origin, c, j):
        return full.at[origin, pl.ds((c * 2 + j) * part, part)]

    def ring(s, j, way):
        origin = at_pos(pos - (s - 1) if way == 0 else pos + (s - 1))
        block = piece(origin, core, j)
        return remote(block, block, rsem.at[0, way, s - 1, j], rsem.at[1, way, s - 1, j],
                      (me, right if way == 0 else left))

    def ways(s, j):
        return (0, 1) if s < half else (j,)

    def source_of(s, way):
        return at_pos(pos - s if way == 0 else pos + s)

    def factor_in(s, j):
        for way in ways(s, j):
            block = piece(source_of(s, way), core, j)
            landed(block, rsem.at[1, way, s - 1, j])
            if s < half and way in ways(s + 1, j):
                go(ring(s + 1, j, way))
            go(remote(block, block, fsem.at[0, way, s - 1, j], fsem.at[1, way, s - 1, j],
                      (sib, col)))

    def factor_all():
        for s in range(1, half + 1):
            for j in range(2):
                for way in ways(s, j):
                    landed(piece(source_of(s, way), 1 - core, j), fsem.at[1, way, s - 1, j])

    for j in range(2):
        for way in ways(1, j):
            go(ring(1, j, way))
    events = [(s, j) for s in range(1, half + 1) for j in range(2)]

    def pump(count):
        for _ in range(min(count, len(events))):
            factor_in(*events.pop(0))

    pump(1)
    for d in range(1, chips):
        send_chunk(1, d)
    pump(1)
    walkers_in(0)

    call[me] = packed
    for k in range(1, nw):
        landed(call.at[(me - k + nw) % nw], crecv.at[k])
    to_smem = pltpu.make_async_copy(call, csm, csem.at[0])
    to_smem.start()
    to_smem.wait()
    wanted = [slot_ref[0, i] for i in range(per)]
    chosen = [jnp.int32(0) for _ in range(per)]
    total = jnp.int32(0)
    for i in range(pop):
        total = total + csm[i // per, 0, i % per]
        for w in range(per):
            chosen[w] = chosen[w] + (total <= wanted[w]).astype(jnp.int32)
    chosen = [jnp.minimum(c, pop - 1) for c in chosen]

    def select(ch, w):
        block = arr[ch][chosen[w]]
        comb_ref[w, ch * nel:(ch + 1) * nel, :] = block
        out = pltpu.make_async_copy(comb_ref.at[w, chunk(ch)], comb_out.at[w, chunk(ch)],
                                    osem.at[w, ch])
        out.start()
        outs.append(out)
        return block.T

    eye = (lax.broadcasted_iota(jnp.int32, (nel, nel), 0)
           == lax.broadcasted_iota(jnp.int32, (nel, nel), 1)).astype(F32)
    walkers_all(0)
    tops = [select(0, w) for w in range(per)]
    for w in range(per):
        ex[w, :nel, :] = eye - tops[w].astype(F32)
        ex[w, nel:, :] = eye

    def newton(steps):
        def step(_, carry):
            for w in range(per):
                both = ex[w]
                high = both.astype(BF16)
                low = (both - high.astype(F32)).astype(BF16)
                prod = (jnp.dot(high, high[:nel], preferred_element_type=F32)
                        + (jnp.dot(high, low[:nel], preferred_element_type=F32)
                           + jnp.dot(low, high[:nel], preferred_element_type=F32)))
                ex[w, :nel, :] = prod[:nel]
                ex[w, nel:, :] = both[nel:] + prod[nel:]
            return carry
        lax.fori_loop(0, steps, step, 0)

    def make_green(ch, flipped):
        for w in range(per):
            green[w * nel:(w + 1) * nel, ch * nel:(ch + 1) * nel] = jnp.dot(
                inv[w], flipped[w], preferred_element_type=F32).astype(BF16)

    def combine(ch):
        walkers_all(ch)
        make_green(ch, [select(ch, w) for w in range(per)])

    third = (NEWTON + 2) // 3
    newton(third)
    pump(1)
    newton(third)
    pump(1)
    walkers_in(1)
    newton(NEWTON - 2 * third)
    for w in range(per):
        inv[w] = ex[w, nel:, :].astype(BF16)
    make_green(0, tops)
    combine(1)
    pump(2)
    for ch in range(2, nch - 1):
        walkers_in(ch)
        combine(ch)
    pump(len(events))
    factor_all()
    lead = rows - nel

    def rotate_lead(l, carry):
        racc[l] = jnp.dot(green[:, :lead], full[l, :lead, :], preferred_element_type=F32)
        return carry

    lax.fori_loop(0, nc, rotate_lead, 0)
    walkers_in(nch - 1)
    combine(nch - 1)

    def rotate_last(l, carry):
        r = racc[l] + jnp.dot(green[:, lead:], full[l, lead:, :], preferred_element_type=F32)
        for w in range(per):
            rt[w, l] = r[w * nel:(w + 1) * nel].astype(BF16)
        return carry

    lax.fori_loop(0, nc, rotate_last, 0)

    for w in range(per):
        lhs = jnp.concatenate([full[l] for l in range(nc)], axis=1)
        rhs = rt[w].reshape(nc * nel, nel)
        grad_ref[w] = -jnp.dot(lhs, rhs, preferred_element_type=F32)
        out = pltpu.make_async_copy(grad_ref.at[w], grad_out.at[w], osem.at[w, nch])
        out.start()
        outs.append(out)
    for out in outs:
        out.wait()
    for copy in sends:
        copy.wait_send()


def body(nw, nc, walkers, counts, slot_copy, factors):
    per, _, rows, nel = walkers.shape
    nch = rows // nel
    pop = nw * per
    vmem = pl.BlockSpec(memory_space=pltpu.VMEM)
    smem = pl.BlockSpec(memory_space=pltpu.SMEM)
    dma = pltpu.SemaphoreType.DMA
    half = nc // 2
    combed, grad = pl.pallas_call(
        functools.partial(kernel, nw, nc),
        out_shape=(
            jax.ShapeDtypeStruct((per, rows, nel), BF16),
            jax.ShapeDtypeStruct((per, rows, nel), F32),
        ),
        in_specs=[smem, smem, vmem, pl.BlockSpec(memory_space=pl.ANY)],
        out_specs=(pl.BlockSpec(memory_space=pl.ANY),) * 2,
        scratch_shapes=[pltpu.VMEM((pop, nel, nel), BF16)] * nch + [
            pltpu.VMEM((nc, rows, nel), BF16),
            pltpu.VMEM((8, 128), jnp.int32),
            pltpu.VMEM((nw, 8, 128), jnp.int32),
            pltpu.SMEM((nw, 8, 128), jnp.int32),
            pltpu.VMEM((per, 2 * nel, nel), F32),
            pltpu.VMEM((per, nel, nel), BF16),
            pltpu.VMEM((per * nel, rows), BF16),
            pltpu.VMEM((nc, per * nel, nel), F32),
            pltpu.VMEM((per, nc, nel, nel), BF16),
            pltpu.VMEM((per, rows, nel), BF16),
            pltpu.VMEM((per, rows, nel), F32),
            dma((per, nch + 1)),
            dma((nw,)),
            dma((nw,)),
            dma((1,)),
            dma((3, nch, 1)),
            dma((4, nch, nw // 2, 2)),
            dma((2, 2, half, 2)),
            dma((2, 2, half, 2)),
        ],
        compiler_params=pltpu.CompilerParams(
            collective_id=0, has_side_effects=True, vmem_limit_bytes=56 << 20),
    )(counts.T, slot_copy.T, factors[0], walkers[:, 0])
    return combed[:, None], grad[:, None]


def solution(mesh):
    nw, nc = mesh.shape["walk"], mesh.shape["chol"]
    wide = P("walk", "chol", None, None)
    flat = P("walk", "chol")
    return jax.shard_map(
        functools.partial(body, nw, nc), mesh=mesh,
        in_specs=(wide, flat, flat, P("chol", None, None)),
        out_specs=(wide, wide), check_vma=False)
```
